32 devices in a mesh: groups: 2 (over y), fsdp: 4 (over z), rows: 2 (over x), tp: 2 (over core).
Axes of the slice: x: 2, y: 2, z: 4, core: 2. Of those that a mesh axis runs over, the one named last changes fastest.
Arguments:
- tokens: bfloat16 [768, 4, 8192], P(('groups', 'fsdp', 'rows'), None, 'tp'), parts along dimension 0, may hold values from -6 to 6
- queries: bfloat16 [768, 4, 32, 128], P(('groups', 'fsdp', 'rows'), None, 'tp'), parts along dimension 0, may hold values from -7 to 7
- kv_cache: bfloat16 [768, 32, 8, 256], P(('groups', 'fsdp', 'rows'), None, 'tp'), parts along dimension 0, may hold values from -6 to 6
- kv_weight: bfloat16 [8192, 8, 256], P('fsdp', 'tp'), may hold values from -0.0625 to 0.0625
- adapter_a: bfloat16 [128, 32, 8192], P(('fsdp', 'rows'), None, 'tp'), may hold values from -0.0625 to 0.0625
- adapter_b: bfloat16 [128, 2, 16, 8, 128], P(('fsdp', 'rows'), None, None, 'tp'), may hold values from -1.5 to 1.5
- adapter_id: int32 [768], P(('groups', 'fsdp', 'rows')), parts along dimension 0, may hold values from 0 to 127, as said below
- kv_len: int32 [768], P(('groups', 'fsdp', 'rows')), parts along dimension 0, may hold values from 2 to 32, as said below
Outputs:
- attended: bfloat16 [768, 4, 32, 128], P(('groups', 'fsdp', 'rows'), None, 'tp'), parts along dimension 0
- new_kv: bfloat16 [768, 4, 8, 256], P(('groups', 'fsdp', 'rows'), None, 'tp'), parts along dimension 0
The draws below stay inside these ranges and needn't reach their ends.
There are 2 independent parts, one for each index of `groups`. The reference program is written for one: setup_inputs(seed, part) draws one part's arguments, and reference() takes and returns one part's arrays. A program takes and returns all parts, laid end to end along the dimension named above; an argument that names none is the same for every part. Nothing has to cross between parts.
Inputs may be any that keep to these rules, and one draw needn't show every extreme that they name: `adapter_id`: adapter a is owned by index a // 16 of fsdp and rows taken together. The rows of one device name adapters of exactly 4 owners, 12 rows for each. `kv_len`: each device has a row of length 32.
All inputs are finite; a program needn't handle non-finite values.
Results may differ from the reference program's by a relative error of at most 0.0055.
Values may be sent and summed in bfloat16 or wider, within the bound.
A program may use at most 128 MiB of HBM per device.

```python
import math
import jax
import jax.numpy as jnp
from jax import lax

D = 8192
KVH = 8
HD = 128
QH = 32
RANK = 16
ADP_DEV = 16
STEPS = 4
ROWS_DEV = 48
CTX = 32
OWNERS = 8
ADAPTERS = 128
ROWS = 384
CAP = 12


def draw_queries(key, part):
    key = jax.random.fold_in(key, 11)
    shape = (ROWS, STEPS, QH, HD)
    values = jnp.clip(jax.random.normal(key, shape, jnp.float32), -6.0, 6.0)
    return values.astype(jnp.bfloat16)


def draw_kv_cache(key, part):
    key = jax.random.fold_in(key, 13)
    shape = (ROWS, CTX, KVH, 2 * HD)
    values = jnp.clip(jax.random.normal(key, shape, jnp.float32), -6.0, 6.0)
    return values.astype(jnp.bfloat16)


def draw_adapter_id(key, part):
    key = jax.random.fold_in(key, 3)
    column = jnp.arange(OWNERS, dtype=jnp.int32)
    noise = jax.random.randint(jax.random.fold_in(key, 1), (OWNERS, OWNERS), 0, 2 ** 20)
    popular = (jax.random.randint(jax.random.fold_in(key, 2), (OWNERS,), 0, 4) == 0).astype(jnp.int32)
    hottest = jax.random.randint(jax.random.fold_in(key, 3), (), 0, OWNERS)
    score = noise + popular[None, :] * 2 ** 18 + (column == hottest).astype(jnp.int32)[None, :] * 2 ** 22
    score = score * OWNERS + column[None, :]
    chosen = lax.top_k(score, ROWS_DEV // CAP)[1].astype(jnp.int32)
    ordered = jnp.repeat(chosen, CAP, axis=1)
    mixing = jax.random.randint(jax.random.fold_in(key, 4), (OWNERS, ROWS_DEV), 0, 2 ** 20)
    mixing = mixing * ROWS_DEV + jnp.arange(ROWS_DEV, dtype=jnp.int32)[None, :]
    shuffle = jnp.argsort(mixing, axis=1)
    owner = jnp.take_along_axis(ordered, shuffle, axis=1)
    local = jax.random.randint(jax.random.fold_in(key, 5), (OWNERS, ROWS_DEV), 0, ADP_DEV)
    return (owner * ADP_DEV + local).reshape(ROWS).astype(jnp.int32)


def draw_kv_len(key, part):
    key = jax.random.fold_in(key, 5)
    lengths = jax.random.randint(jax.random.fold_in(key, 1), (OWNERS, ROWS_DEV), 2, CTX + 1)
    longest = jax.random.randint(jax.random.fold_in(key, 2), (OWNERS, 1), 0, ROWS_DEV)
    lengths = jnp.where(jnp.arange(ROWS_DEV, dtype=jnp.int32)[None, :] == longest, CTX, lengths)
    return lengths.reshape(ROWS).astype(jnp.int32)


def steps_of(stream_key, shape, shards, low, largest):
    level = 1.0
    for dim, parts in shards:
        steps = jax.random.uniform(jax.random.fold_in(jax.random.fold_in(stream_key, 6), dim), (parts,), jnp.float32, low / len(shards), largest / len(shards))
        level = level * jnp.repeat(jnp.exp(steps), shape[dim] // parts).reshape((-1,) + (1,) * (len(shape) - 1 - dim))
    return level


def centred(rng, dims, deviation, bound, cuts=(), kind=jnp.bfloat16):
    gain = steps_of(rng, dims, cuts, -0.22, 0.18) if cuts else 1.0
    entries = jax.random.normal(rng, dims, jnp.float32) * deviation * gain
    return jnp.minimum(jnp.maximum(entries, -bound), bound).astype(kind)


def setup_inputs(seed: int = 0, part: int = 0) -> dict:
    streams_of = jax.random.split(jax.random.key(seed), 9)
    part_splits = jax.random.split(jax.random.fold_in(streams_of[8], part), 9)
    return {
        "tokens": centred(part_splits[0], (ROWS, STEPS, D), 1.0, 6.0, ((0, 8), (2, 2))),
        "queries": draw_queries(jax.random.fold_in(jax.random.fold_in(streams_of[8], part), 71), part),
        "kv_cache": draw_kv_cache(jax.random.fold_in(jax.random.fold_in(streams_of[8], part), 71), part),
        "kv_weight": centred(streams_of[3], (D, KVH, 2 * HD), D ** -0.5, 0.0625, ((0, 4), (1, 2))),
        "adapter_a": centred(streams_of[4], (ADAPTERS, 2 * RANK, D), D ** -0.5, 0.0625, ((0, 8), (2, 2))),
        "adapter_b": centred(streams_of[5], (ADAPTERS, 2, RANK, KVH, HD), RANK ** -0.5, 1.5, ((0, 8), (3, 2))),
        "adapter_id": draw_adapter_id(jax.random.fold_in(jax.random.fold_in(streams_of[8], part), 71), part),
        "kv_len": draw_kv_len(jax.random.fold_in(jax.random.fold_in(streams_of[8], part), 71), part),
    }


low_rank_scale = 0.5
rope_base = 500000.0

def rotate_keys(summed, positions):
    depth = summed.shape[-1] // 2
    half = depth // 2
    index = jnp.arange(half, dtype=jnp.int32).astype(jnp.float32)
    inverse = jnp.exp(index * (-2.0 * math.log(rope_base) / depth))
    angle = positions[..., None] * inverse
    cosine = jnp.cos(angle)[:, :, None, :]
    sine = jnp.sin(angle)[:, :, None, :]
    first = summed[..., :half]
    second = summed[..., half:depth]
    return jnp.concatenate([first * cosine - second * sine, second * cosine + first * sine, summed[..., depth:]], axis=-1)

def attend(queries, cache, fresh, lengths):
    batch, decode_steps, query_heads, depth = queries.shape
    kv_heads = cache.shape[2]
    context = cache.shape[1]
    grouped = queries.reshape(batch, decode_steps, kv_heads, query_heads // kv_heads, depth).astype(jnp.float32)
    scale = 1.0 / math.sqrt(depth)
    older = jnp.einsum('rsgqd,rpgd->rsgqp', grouped, cache[..., :depth].astype(jnp.float32)) * scale
    newer = jnp.einsum('rsgqd,rtgd->rsgqt', grouped, fresh[..., :depth].astype(jnp.float32)) * scale
    visible_old = jnp.arange(context, dtype=jnp.int32)[None, :] < lengths[:, None]
    visible_new = jnp.arange(decode_steps, dtype=jnp.int32)[None, :] <= jnp.arange(decode_steps, dtype=jnp.int32)[:, None]
    older = jnp.where(visible_old[:, None, None, None, :], older, -jnp.inf)
    newer = jnp.where(visible_new[None, :, None, None, :], newer, -jnp.inf)
    scores = jnp.concatenate([older, newer], axis=-1)
    top = lax.optimization_barrier(jnp.max(scores, axis=-1, keepdims=True))
    weights = jnp.exp(scores - top)
    weights = (weights / lax.optimization_barrier(jnp.sum(weights, axis=-1, keepdims=True))).astype(jnp.bfloat16).astype(jnp.float32)
    mixed = jnp.einsum('rsgqp,rpgd->rsgqd', weights[..., :context], cache[..., depth:].astype(jnp.float32))
    mixed = mixed + jnp.einsum('rsgqt,rtgd->rsgqd', weights[..., context:], fresh[..., depth:].astype(jnp.float32))
    return mixed.reshape(batch, decode_steps, query_heads, depth).astype(jnp.bfloat16)

def adapter_terms(tokens, adapter_id, adapter_a, adapter_b):
    blocks_x = tokens.reshape(OWNERS, ROWS_DEV, STEPS, D)
    blocks_id = adapter_id.reshape(OWNERS, ROWS_DEV)

    def one_block(payload):
        block_rows, names = payload
        down = jnp.take(adapter_a, names, axis=0).astype(jnp.float32)
        position_coords = jnp.einsum('bsd,brd->bsr', block_rows.astype(jnp.float32), down)
        position_coords = position_coords.astype(jnp.bfloat16).astype(jnp.float32).reshape(ROWS_DEV, STEPS, 2, RANK)
        up_projection = jnp.take(adapter_b, names, axis=0).astype(jnp.float32)
        adapter_update = jnp.einsum('ptau,pauoy->ptoay', position_coords, up_projection) * low_rank_scale
        return adapter_update.reshape(ROWS_DEV, STEPS, KVH, 2 * HD).astype(jnp.bfloat16)
    result = lax.map(one_block, (blocks_x, blocks_id))
    return result.reshape(ROWS, STEPS, KVH, 2 * HD)

def reference(tokens, queries, kv_cache, kv_weight, adapter_a, adapter_b, adapter_id, kv_len):
    base_terms = jnp.dot(tokens.reshape(ROWS * STEPS, D), kv_weight.reshape(D, KVH * 2 * HD), preferred_element_type=jnp.float32)
    base_terms = base_terms.reshape(ROWS, STEPS, KVH, 2 * HD)
    adapter_update = adapter_terms(tokens, adapter_id, adapter_a, adapter_b)
    summed = base_terms + adapter_update.astype(jnp.float32)
    positions = (kv_len[:, None] + jnp.arange(STEPS, dtype=jnp.int32)[None, :]).astype(jnp.float32)
    new_kv = rotate_keys(summed, positions).astype(jnp.bfloat16)
    attended = attend(queries, kv_cache, new_kv, kv_len)
    return (attended, new_kv)
```

```python
import functools
import math

import jax
import jax.numpy as jnp
from jax import lax
from jax.experimental import pallas as pl
from jax.experimental.pallas import tpu as pltpu
from jax.sharding import PartitionSpec as P

ADP_DEV = 16
CHUNKS = 4
MESH = pl.DeviceIdType.MESH

low_rank_scale = 0.5
rope_base = 500000.0


def rotate_keys(summed, positions):
    depth = summed.shape[-1] // 2
    half = depth // 2
    index = jnp.arange(half, dtype=jnp.int32).astype(jnp.float32)
    inverse = jnp.exp(index * (-2.0 * math.log(rope_base) / depth))
    angle = positions[..., None] * inverse
    cosine = jnp.cos(angle)[:, :, None, :]
    sine = jnp.sin(angle)[:, :, None, :]
    first = summed[..., :half]
    second = summed[..., half:depth]
    return jnp.concatenate(
        [first * cosine - second * sine, second * cosine + first * sine, summed[..., depth:]],
        axis=-1,
    )


def attend(queries, cache, fresh, lengths):
    batch, decode_steps, query_heads, depth = queries.shape
    kv_heads = cache.shape[2]
    context = cache.shape[1]
    grouped = queries.reshape(batch, decode_steps, kv_heads, query_heads // kv_heads, depth)
    scale = 1.0 / math.sqrt(depth)
    older = (
        jnp.einsum(
            "rsgqd,rpgd->rsgqp", grouped, cache[..., :depth], preferred_element_type=jnp.float32
        )
        * scale
    )
    newer = (
        jnp.einsum(
            "rsgqd,rtgd->rsgqt", grouped, fresh[..., :depth], preferred_element_type=jnp.float32
        )
        * scale
    )
    visible_old = jnp.arange(context, dtype=jnp.int32)[None, :] < lengths[:, None]
    visible_new = (
        jnp.arange(decode_steps, dtype=jnp.int32)[None, :]
        <= jnp.arange(decode_steps, dtype=jnp.int32)[:, None]
    )
    older = jnp.where(visible_old[:, None, None, None, :], older, -jnp.inf)
    newer = jnp.where(visible_new[None, :, None, None, :], newer, -jnp.inf)
    scores = jnp.concatenate([older, newer], axis=-1)
    top = jnp.max(scores, axis=-1, keepdims=True)
    weights = jnp.exp(scores - top)
    weights = (weights / jnp.sum(weights, axis=-1, keepdims=True)).astype(jnp.bfloat16)
    mixed = jnp.einsum(
        "rsgqp,rpgd->rsgqd",
        weights[..., :context],
        cache[..., depth:],
        preferred_element_type=jnp.float32,
    )
    mixed = mixed + jnp.einsum(
        "rsgqt,rtgd->rsgqd",
        weights[..., context:],
        fresh[..., depth:],
        preferred_element_type=jnp.float32,
    )
    return mixed.reshape(batch, decode_steps, query_heads, depth).astype(jnp.bfloat16)


def gather_kernel(
    n, m, tok, a, b, ids, tok_all, slices, a_all, b_all, ids_all,
    own_sem, right_send, left_send, tok_recv, core_send, core_recv,
    x_send, x_recv, id_send, id_recv,
):
    f = lax.axis_index("fsdp")
    r = lax.axis_index("rows")
    t = lax.axis_index("tp")
    rows, half = tok.shape
    part = rows // CHUNKS
    width = slices.shape[2]
    per_core = half // width
    holds = t == f // per_core
    column = pl.multiple_of(lax.rem(f, per_core) * width, width)

    barrier = pltpu.get_barrier_semaphore()
    for k in range(1, n):
        pl.semaphore_signal(
            barrier, inc=1, device_id={"fsdp": lax.rem(f + k, n)}, device_id_type=MESH
        )
    for k in range(1, m):
        pl.semaphore_signal(
            barrier, inc=1, device_id={"rows": lax.rem(r + k, m)}, device_id_type=MESH
        )
    pl.semaphore_signal(barrier, inc=1, device_id={"tp": 1 - t}, device_id_type=MESH)
    pl.semaphore_wait(barrier, n + m - 1)

    def piece(c):
        return pl.ds(c * part, part)

    def along(source, src, c, to, sems):
        return pltpu.make_async_remote_copy(
            src_ref=source,
            dst_ref=tok_all.at[src, piece(c)],
            send_sem=sems.at[src, c],
            recv_sem=tok_recv.at[src, c],
            device_id={"fsdp": to},
            device_id_type=MESH,
        )

    def across(source, src, c):
        return pltpu.make_async_remote_copy(
            src_ref=source,
            dst_ref=slices.at[src, piece(c)],
            send_sem=core_send.at[src, c],
            recv_sem=core_recv.at[src, c],
            device_id={"tp": 1 - t},
            device_id_type=MESH,
        )

    def keep(source, src, c):
        return pltpu.make_async_copy(source, slices.at[src, piece(c)], core_recv.at[src, c])

    def id_copy(k):
        return pltpu.make_async_remote_copy(
            src_ref=ids,
            dst_ref=ids_all.at[f],
            send_sem=id_send.at[k],
            recv_sem=id_recv.at[k],
            device_id={"fsdp": lax.rem(f + k, n)},
            device_id_type=MESH,
        )

    def x_copy(k, which):
        source, target = ((a, a_all), (b, b_all))[which]
        return pltpu.make_async_remote_copy(
            src_ref=source,
            dst_ref=target.at[r],
            send_sem=x_send.at[which, k],
            recv_sem=x_recv.at[which, k],
            device_id={"rows": lax.rem(r + k, m)},
            device_id_type=MESH,
        )

    for c in range(CHUNKS):
        @pl.when(f < n - 1)
        def _():
            along(tok.at[piece(c)], f, c, f + 1, right_send).start()

        @pl.when(f > 0)
        def _():
            along(tok.at[piece(c)], f, c, f - 1, left_send).start()

    for k in range(1, n):
        id_copy(k).start()
    for k in range(1, m):
        for which in range(2):
            x_copy(k, which).start()
    locals_ = [
        pltpu.make_async_copy(tok, tok_all.at[f], own_sem.at[0]),
        pltpu.make_async_copy(a, a_all.at[r], own_sem.at[1]),
        pltpu.make_async_copy(b, b_all.at[r], own_sem.at[2]),
        pltpu.make_async_copy(ids, ids_all.at[f], own_sem.at[3]),
    ]
    for copy in locals_:
        copy.start()
    for c in range(CHUNKS):
        @pl.when(holds)
        def _():
            across(tok.at[piece(c), pl.ds(column, width)], f, c).start()
            keep(tok.at[piece(c), pl.ds(column, width)], f, c).start()

    for d in range(1, n):
        for c in range(CHUNKS):
            @pl.when(f >= d)
            def _():
                src = f - d
                along(tok.at[piece(c)], src, c, f, right_send).wait_recv()

                @pl.when(f < n - 1)
                def _():
                    along(tok_all.at[src, piece(c)], src, c, f + 1, right_send).start()

                @pl.when(holds)
                def _():
                    across(tok_all.at[src, piece(c), pl.ds(column, width)], src, c).start()
                    keep(tok_all.at[src, piece(c), pl.ds(column, width)], src, c).start()

            @pl.when(f + d < n)
            def _():
                src = f + d
                along(tok.at[piece(c)], src, c, f, left_send).wait_recv()

                @pl.when(f > 0)
                def _():
                    along(tok_all.at[src, piece(c)], src, c, f - 1, left_send).start()

                @pl.when(holds)
                def _():
                    across(tok_all.at[src, piece(c), pl.ds(column, width)], src, c).start()
                    keep(tok_all.at[src, piece(c), pl.ds(column, width)], src, c).start()

    for copy in locals_:
        copy.wait()
    for k in range(1, n):
        id_copy(k).wait()
    for k in range(1, m):
        for which in range(2):
            x_copy(k, which).wait()
    for src in range(n):
        for c in range(CHUNKS):
            @pl.when(jnp.logical_and(src <= f, f < n - 1))
            def _():
                along(tok.at[piece(c)], src, c, f, right_send).wait_send()

            @pl.when(jnp.logical_and(src >= f, f > 0))
            def _():
                along(tok.at[piece(c)], src, c, f, left_send).wait_send()

            @pl.when(holds)
            def _():
                across(tok.at[piece(c), pl.ds(column, width)], src, c).wait_send()
                keep(tok.at[piece(c), pl.ds(column, width)], src, c).wait()

            @pl.when(jnp.logical_not(holds))
            def _():
                across(tok.at[piece(c), pl.ds(column, width)], src, c).wait_recv()


def gather(tok, a, b, ids, n, m, width):
    shape = jax.ShapeDtypeStruct
    anywhere = pl.BlockSpec(memory_space=pl.ANY)
    dma = pltpu.SemaphoreType.DMA
    return pl.pallas_call(
        functools.partial(gather_kernel, n, m),
        out_shape=(
            shape((n,) + tok.shape, tok.dtype),
            shape((n, tok.shape[0], width), tok.dtype),
            shape((m,) + a.shape, a.dtype),
            shape((m,) + b.shape, b.dtype),
            shape((n,) + ids.shape, ids.dtype),
        ),
        in_specs=[anywhere] * 4,
        out_specs=[anywhere] * 5,
        scratch_shapes=[
            dma((4,)),
            dma((n, CHUNKS)),
            dma((n, CHUNKS)),
            dma((n, CHUNKS)),
            dma((n, CHUNKS)),
            dma((n, CHUNKS)),
            dma((2, m)),
            dma((2, m)),
            dma((n,)),
            dma((n,)),
        ],
        compiler_params=pltpu.CompilerParams(collective_id=0, has_side_effects=True),
    )(tok, a, b, ids)


def exchange_kernel(n, parts, out, send, recv):
    f = lax.axis_index("fsdp")
    barrier = pltpu.get_barrier_semaphore()
    for k in range(1, n):
        pl.semaphore_signal(
            barrier, inc=1, device_id={"fsdp": lax.rem(f + k, n)}, device_id_type=MESH
        )
    pl.semaphore_wait(barrier, n - 1)

    def copy(k):
        to = lax.rem(f + k, n)
        return pltpu.make_async_remote_copy(
            src_ref=parts.at[to],
            dst_ref=out.at[f],
            send_sem=send.at[k],
            recv_sem=recv.at[k],
            device_id={"fsdp": to},
            device_id_type=MESH,
        )

    for k in range(1, n):
        copy(k).start()
    for k in range(1, n):
        copy(k).wait()


def exchange(parts, n):
    anywhere = pl.BlockSpec(memory_space=pl.ANY)
    return pl.pallas_call(
        functools.partial(exchange_kernel, n),
        out_shape=jax.ShapeDtypeStruct(parts.shape, parts.dtype),
        in_specs=[anywhere],
        out_specs=anywhere,
        scratch_shapes=[pltpu.SemaphoreType.DMA((n,)), pltpu.SemaphoreType.DMA((n,))],
        compiler_params=pltpu.CompilerParams(collective_id=1, has_side_effects=True),
    )(parts)


def local(tokens, queries, kv_cache, kv_weight, adapter_a, adapter_b, adapter_id, kv_len):
    n = lax.axis_size("fsdp")
    m = lax.axis_size("rows")
    f = lax.axis_index("fsdp")
    rows_dev, decode_steps, half_width = tokens.shape
    width, heads, pair = kv_weight.shape
    rank = adapter_b.shape[2]
    count = rows_dev * decode_steps
    known = m * ADP_DEV

    flat = tokens.reshape(count, half_width)
    weight = kv_weight.reshape(width, heads * pair)
    down = adapter_a.reshape(ADP_DEV * 2 * rank, half_width)
    up = adapter_b.reshape(ADP_DEV * 2 * rank, heads * (pair // 2))
    lanes = -(-rows_dev // 128) * 128
    ids = jnp.broadcast_to(jnp.pad(adapter_id, (0, lanes - rows_dev))[None, :], (8, lanes))
    tok_all, slices, a_all, b_all, ids_all = gather(flat, down, up, ids, n, m, width)

    names = ids_all[:, 0, :rows_dev].reshape(n * rows_dev) - f * known
    chosen = names[:, None] == jnp.arange(known, dtype=jnp.int32)
    chosen = jnp.broadcast_to(chosen[:, None, :], (n * rows_dev, decode_steps, known))
    chosen = chosen.reshape(n * count, known)
    projected = lax.dot_general(
        tok_all.reshape(n * count, half_width),
        a_all.reshape(known * 2 * rank, half_width),
        (((1,), (1,)), ((), ())),
        preferred_element_type=jnp.float32,
    )
    coords = jnp.sum(
        jnp.where(chosen[:, :, None], projected.reshape(n * count, known, 2 * rank), 0.0), axis=1
    )
    coords = lax.psum(coords, "tp").astype(jnp.bfloat16)
    spread = jnp.where(chosen[:, :, None], coords[:, None, :], jnp.bfloat16(0))
    spread = spread.reshape(n * count, known, 2, rank)
    delta = jnp.einsum(
        "takr,akrhd->thkd",
        spread,
        b_all.reshape(known, 2, rank, heads, pair // 2),
        preferred_element_type=jnp.float32,
    )
    delta = (delta * low_rank_scale).astype(jnp.bfloat16).reshape(n * count, heads * pair)
    partial = jnp.dot(
        slices.reshape(n * count, width), weight, preferred_element_type=jnp.float32
    )
    partial = (partial + delta.astype(jnp.float32)).reshape(n, count, heads * pair)
    others = exchange(partial.astype(jnp.bfloat16), n)
    mine = lax.dynamic_index_in_dim(partial, f, 0, keepdims=False)
    slot = jnp.arange(n, dtype=jnp.int32)[:, None, None]
    summed = mine + jnp.sum(jnp.where(slot == f, 0.0, others.astype(jnp.float32)), axis=0)
    summed = summed.reshape(rows_dev, decode_steps, heads, pair)
    positions = (kv_len[:, None] + jnp.arange(decode_steps, dtype=jnp.int32)[None, :]).astype(
        jnp.float32
    )
    new_kv = rotate_keys(summed, positions).astype(jnp.bfloat16)
    attended = attend(queries, kv_cache, new_kv, kv_len)
    return (attended, new_kv)


def solution(mesh):
    placed = (
        P(("groups", "fsdp", "rows"), None, "tp"),
        P(("groups", "fsdp", "rows"), None, "tp", None),
        P(("groups", "fsdp", "rows"), None, "tp", None),
        P("fsdp", "tp", None),
        P(("fsdp", "rows"), None, "tp"),
        P(("fsdp", "rows"), None, None, "tp", None),
        P(("groups", "fsdp", "rows")),
        P(("groups", "fsdp", "rows")),
    )
    return jax.shard_map(
        local,
        mesh=mesh,
        in_specs=placed,
        out_specs=(
            P(("groups", "fsdp", "rows"), None, "tp", None),
            P(("groups", "fsdp", "rows"), None, "tp", None),
        ),
        check_vma=False,
    )
```

```python
import functools
import math

import jax
import jax.numpy as jnp
from jax import lax
from jax.experimental import pallas as pl
from jax.experimental.pallas import tpu as pltpu
from jax.sharding import PartitionSpec as P

ADP_DEV = 16
CHUNKS = 4
MESH = pl.DeviceIdType.MESH

low_rank_scale = 0.5
rope_base = 500000.0


def rotate_keys(summed, positions):
    depth = summed.shape[-1] // 2
    half = depth // 2
    index = jnp.arange(half, dtype=jnp.int32).astype(jnp.float32)
    inverse = jnp.exp(index * (-2.0 * math.log(rope_base) / depth))
    angle = positions[..., None] * inverse
    cosine = jnp.cos(angle)[:, :, None, :]
    sine = jnp.sin(angle)[:, :, None, :]
    first = summed[..., :half]
    second = summed[..., half:depth]
    return jnp.concatenate(
        [first * cosine - second * sine, second * cosine + first * sine, summed[..., depth:]],
        axis=-1,
    )


def attend(queries, cache, fresh, lengths):
    batch, decode_steps, query_heads, depth = queries.shape
    kv_heads = cache.shape[2]
    context = cache.shape[1]
    grouped = queries.reshape(batch, decode_steps, kv_heads, query_heads // kv_heads, depth)
    scale = 1.0 / math.sqrt(depth)
    older = (
        jnp.einsum(
            "rsgqd,rpgd->rsgqp", grouped, cache[..., :depth], preferred_element_type=jnp.float32
        )
        * scale
    )
    newer = (
        jnp.einsum(
            "rsgqd,rtgd->rsgqt", grouped, fresh[..., :depth], preferred_element_type=jnp.float32
        )
        * scale
    )
    visible_old = jnp.arange(context, dtype=jnp.int32)[None, :] < lengths[:, None]
    visible_new = (
        jnp.arange(decode_steps, dtype=jnp.int32)[None, :]
        <= jnp.arange(decode_steps, dtype=jnp.int32)[:, None]
    )
    older = jnp.where(visible_old[:, None, None, None, :], older, -jnp.inf)
    newer = jnp.where(visible_new[None, :, None, None, :], newer, -jnp.inf)
    scores = jnp.concatenate([older, newer], axis=-1)
    top = jnp.max(scores, axis=-1, keepdims=True)
    weights = jnp.exp(scores - top)
    weights = (weights / jnp.sum(weights, axis=-1, keepdims=True)).astype(jnp.bfloat16)
    mixed = jnp.einsum(
        "rsgqp,rpgd->rsgqd",
        weights[..., :context],
        cache[..., depth:],
        preferred_element_type=jnp.float32,
    )
    mixed = mixed + jnp.einsum(
        "rsgqt,rtgd->rsgqd",
        weights[..., context:],
        fresh[..., depth:],
        preferred_element_type=jnp.float32,
    )
    return mixed.reshape(batch, decode_steps, query_heads, depth).astype(jnp.bfloat16)


def gather_kernel(
    n, m, tok, a, b, ids, tok_all, slices, a_all, b_all, ids_all,
    tok_v, a_v, b_v, ids_v, in_sem, own_sem, right_send, left_send, tok_recv, core_send, core_recv,
    x_send, x_recv, id_send, id_recv,
):
    f = lax.axis_index("fsdp")
    r = lax.axis_index("rows")
    t = lax.axis_index("tp")
    rows, half = tok.shape
    part = rows // CHUNKS
    width = slices.shape[2]
    per_core = half // width
    holds = t == f // per_core
    column = pl.multiple_of(lax.rem(f, per_core) * width, width)

    barrier = pltpu.get_barrier_semaphore()
    for k in range(1, n):
        pl.semaphore_signal(
            barrier, inc=1, device_id={"fsdp": lax.rem(f + k, n)}, device_id_type=MESH
        )
    for k in range(1, m):
        pl.semaphore_signal(
            barrier, inc=1, device_id={"rows": lax.rem(r + k, m)}, device_id_type=MESH
        )
    pl.semaphore_signal(barrier, inc=1, device_id={"tp": 1 - t}, device_id_type=MESH)
    pl.semaphore_wait(barrier, n + m - 1)

    def piece(c):
        return pl.ds(c * part, part)

    def along(source, src, c, to, sems):
        return pltpu.make_async_remote_copy(
            src_ref=source,
            dst_ref=tok_all.at[src, piece(c)],
            send_sem=sems.at[src, c],
            recv_sem=tok_recv.at[src, c],
            device_id={"fsdp": to},
            device_id_type=MESH,
        )

    def across(source, src, c):
        return pltpu.make_async_remote_copy(
            src_ref=source,
            dst_ref=slices.at[src, piece(c)],
            send_sem=core_send.at[src, c],
            recv_sem=core_recv.at[src, c],
            device_id={"tp": 1 - t},
            device_id_type=MESH,
        )

    def keep(source, src, c):
        return pltpu.make_async_copy(source, slices.at[src, piece(c)], core_recv.at[src, c])

    def id_copy(k):
        return pltpu.make_async_remote_copy(
            src_ref=ids,
            dst_ref=ids_all.at[f],
            send_sem=id_send.at[k],
            recv_sem=id_recv.at[k],
            device_id={"fsdp": lax.rem(f + k, n)},
            device_id_type=MESH,
        )

    def x_copy(k, which):
        source, target = ((a, a_all), (b, b_all))[which]
        return pltpu.make_async_remote_copy(
            src_ref=source,
            dst_ref=target.at[r],
            send_sem=x_send.at[which, k],
            recv_sem=x_recv.at[which, k],
            device_id={"rows": lax.rem(r + k, m)},
            device_id_type=MESH,
        )

    for c in range(CHUNKS):
        @pl.when(f < n - 1)
        def _():
            along(tok.at[piece(c)], f, c, f + 1, right_send).start()

        @pl.when(f > 0)
        def _():
            along(tok.at[piece(c)], f, c, f - 1, left_send).start()

    for k in range(1, n):
        id_copy(k).start()
    for k in range(1, m):
        for which in range(2):
            x_copy(k, which).start()
    held = ((tok, tok_v), (a, a_v), (b, b_v), (ids, ids_v))
    inward = [pltpu.make_async_copy(x, v, in_sem.at[i]) for i, (x, v) in enumerate(held)]
    for copy in inward:
        copy.start()
    locals_ = [
        pltpu.make_async_copy(tok_v, tok_all.at[f], own_sem.at[0]),
        pltpu.make_async_copy(a_v, a_all.at[r], own_sem.at[1]),
        pltpu.make_async_copy(b_v, b_all.at[r], own_sem.at[2]),
        pltpu.make_async_copy(ids_v, ids_all.at[f], own_sem.at[3]),
    ]
    for first, second in zip(inward, locals_):
        first.wait()
        second.start()
    for c in range(CHUNKS):
        @pl.when(holds)
        def _():
            across(tok.at[piece(c), pl.ds(column, width)], f, c).start()
            keep(tok_v.at[piece(c), pl.ds(column, width)], f, c).start()

    for d in range(1, n):
        for c in range(CHUNKS):
            @pl.when(f >= d)
            def _():
                src = f - d
                along(tok.at[piece(c)], src, c, f, right_send).wait_recv()

                @pl.when(f < n - 1)
                def _():
                    along(tok_all.at[src, piece(c)], src, c, f + 1, right_send).start()

                @pl.when(holds)
                def _():
                    across(tok_all.at[src, piece(c), pl.ds(column, width)], src, c).start()
                    keep(tok_all.at[src, piece(c), pl.ds(column, width)], src, c).start()

            @pl.when(f + d < n)
            def _():
                src = f + d
                along(tok.at[piece(c)], src, c, f, left_send).wait_recv()

                @pl.when(f > 0)
                def _():
                    along(tok_all.at[src, piece(c)], src, c, f - 1, left_send).start()

                @pl.when(holds)
                def _():
                    across(tok_all.at[src, piece(c), pl.ds(column, width)], src, c).start()
                    keep(tok_all.at[src, piece(c), pl.ds(column, width)], src, c).start()

    for copy in locals_:
        copy.wait()
    for k in range(1, n):
        id_copy(k).wait()
    for k in range(1, m):
        for which in range(2):
            x_copy(k, which).wait()
    for src in range(n):
        for c in range(CHUNKS):
            @pl.when(jnp.logical_and(src <= f, f < n - 1))
            def _():
                along(tok.at[piece(c)], src, c, f, right_send).wait_send()

            @pl.when(jnp.logical_and(src >= f, f > 0))
            def _():
                along(tok.at[piece(c)], src, c, f, left_send).wait_send()

            @pl.when(holds)
            def _():
                across(tok.at[piece(c), pl.ds(column, width)], src, c).wait_send()
                keep(tok.at[piece(c), pl.ds(column, width)], src, c).wait()

            @pl.when(jnp.logical_not(holds))
            def _():
                across(tok.at[piece(c), pl.ds(column, width)], src, c).wait_recv()


def gather(tok, a, b, ids, n, m, width):
    shape = jax.ShapeDtypeStruct
    anywhere = pl.BlockSpec(memory_space=pl.ANY)
    dma = pltpu.SemaphoreType.DMA
    return pl.pallas_call(
        functools.partial(gather_kernel, n, m),
        out_shape=(
            shape((n,) + tok.shape, tok.dtype),
            shape((n, tok.shape[0], width), tok.dtype),
            shape((m,) + a.shape, a.dtype),
            shape((m,) + b.shape, b.dtype),
            shape((n,) + ids.shape, ids.dtype),
        ),
        in_specs=[anywhere] * 4,
        out_specs=[anywhere] * 5,
        scratch_shapes=[pltpu.VMEM(x.shape, x.dtype) for x in (tok, a, b, ids)]
        + [
            dma((4,)),
            dma((4,)),
            dma((n, CHUNKS)),
            dma((n, CHUNKS)),
            dma((n, CHUNKS)),
            dma((n, CHUNKS)),
            dma((n, CHUNKS)),
            dma((2, m)),
            dma((2, m)),
            dma((n,)),
            dma((n,)),
        ],
        compiler_params=pltpu.CompilerParams(
            collective_id=0, has_side_effects=True, vmem_limit_bytes=32 * 2**20
        ),
    )(tok, a, b, ids)


def exchange_kernel(n, parts, out, send, recv):
    f = lax.axis_index("fsdp")
    barrier = pltpu.get_barrier_semaphore()
    for k in range(1, n):
        pl.semaphore_signal(
            barrier, inc=1, device_id={"fsdp": lax.rem(f + k, n)}, device_id_type=MESH
        )
    pl.semaphore_wait(barrier, n - 1)

    def copy(k):
        to = lax.rem(f + k, n)
        return pltpu.make_async_remote_copy(
            src_ref=parts.at[to],
            dst_ref=out.at[f],
            send_sem=send.at[k],
            recv_sem=recv.at[k],
            device_id={"fsdp": to},
            device_id_type=MESH,
        )

    for k in range(1, n):
        copy(k).start()
    for k in range(1, n):
        copy(k).wait()


def exchange(parts, n):
    anywhere = pl.BlockSpec(memory_space=pl.ANY)
    return pl.pallas_call(
        functools.partial(exchange_kernel, n),
        out_shape=jax.ShapeDtypeStruct(parts.shape, parts.dtype),
        in_specs=[anywhere],
        out_specs=anywhere,
        scratch_shapes=[pltpu.SemaphoreType.DMA((n,)), pltpu.SemaphoreType.DMA((n,))],
        compiler_params=pltpu.CompilerParams(collective_id=1, has_side_effects=True),
    )(parts)


def local(tokens, queries, kv_cache, kv_weight, adapter_a, adapter_b, adapter_id, kv_len):
    n = lax.axis_size("fsdp")
    m = lax.axis_size("rows")
    f = lax.axis_index("fsdp")
    rows_dev, decode_steps, half_width = tokens.shape
    width, heads, pair = kv_weight.shape
    rank = adapter_b.shape[2]
    count = rows_dev * decode_steps
    known = m * ADP_DEV

    flat = tokens.reshape(count, half_width)
    weight = kv_weight.reshape(width, heads * pair)
    down = adapter_a.reshape(ADP_DEV * 2 * rank, half_width)
    up = adapter_b.reshape(ADP_DEV * 2 * rank, heads * (pair // 2))
    lanes = -(-rows_dev // 128) * 128
    ids = jnp.broadcast_to(jnp.pad(adapter_id, (0, lanes - rows_dev))[None, :], (8, lanes))
    tok_all, slices, a_all, b_all, ids_all = gather(flat, down, up, ids, n, m, width)

    names = ids_all[:, 0, :rows_dev].reshape(n * rows_dev) - f * known
    chosen = names[:, None] == jnp.arange(known, dtype=jnp.int32)
    chosen = jnp.broadcast_to(chosen[:, None, :], (n * rows_dev, decode_steps, known))
    chosen = chosen.reshape(n * count, known)
    projected = lax.dot_general(
        tok_all.reshape(n * count, half_width),
        a_all.reshape(known * 2 * rank, half_width),
        (((1,), (1,)), ((), ())),
        preferred_element_type=jnp.float32,
    )
    coords = jnp.sum(
        jnp.where(chosen[:, :, None], projected.reshape(n * count, known, 2 * rank), 0.0), axis=1
    )
    coords = lax.psum(coords, "tp").astype(jnp.bfloat16)
    spread = jnp.where(chosen[:, :, None], coords[:, None, :], jnp.bfloat16(0))
    spread = spread.reshape(n * count, known, 2, rank)
    delta = jnp.einsum(
        "takr,akrhd->thkd",
        spread,
        b_all.reshape(known, 2, rank, heads, pair // 2),
        preferred_element_type=jnp.float32,
    )
    delta = (delta * low_rank_scale).astype(jnp.bfloat16).reshape(n * count, heads * pair)
    partial = jnp.dot(
        slices.reshape(n * count, width), weight, preferred_element_type=jnp.float32
    )
    partial = (partial + delta.astype(jnp.float32)).reshape(n, count, heads * pair)
    others = exchange(partial.astype(jnp.bfloat16), n)
    mine = lax.dynamic_index_in_dim(partial, f, 0, keepdims=False)
    slot = jnp.arange(n, dtype=jnp.int32)[:, None, None]
    summed = mine + jnp.sum(jnp.where(slot == f, 0.0, others.astype(jnp.float32)), axis=0)
    summed = summed.reshape(rows_dev, decode_steps, heads, pair)
    positions = (kv_len[:, None] + jnp.arange(decode_steps, dtype=jnp.int32)[None, :]).astype(
        jnp.float32
    )
    new_kv = rotate_keys(summed, positions).astype(jnp.bfloat16)
    attended = attend(queries, kv_cache, new_kv, kv_len)
    return (attended, new_kv)


def solution(mesh):
    placed = (
        P(("groups", "fsdp", "rows"), None, "tp"),
        P(("groups", "fsdp", "rows"), None, "tp", None),
        P(("groups", "fsdp", "rows"), None, "tp", None),
        P("fsdp", "tp", None),
        P(("fsdp", "rows"), None, "tp"),
        P(("fsdp", "rows"), None, None, "tp", None),
        P(("groups", "fsdp", "rows")),
        P(("groups", "fsdp", "rows")),
    )
    return jax.shard_map(
        local,
        mesh=mesh,
        in_specs=placed,
        out_specs=(
            P(("groups", "fsdp", "rows"), None, "tp", None),
            P(("groups", "fsdp", "rows"), None, "tp", None),
        ),
        check_vma=False,
    )
```

```python
import functools
import math

import jax
import jax.numpy as jnp
from jax import lax
from jax.experimental import pallas as pl
from jax.experimental.pallas import tpu as pltpu
from jax.sharding import PartitionSpec as P

ADP_DEV = 16
CHUNKS = 4
MESH = pl.DeviceIdType.MESH

low_rank_scale = 0.5
rope_base = 500000.0


def rotate_keys(summed, positions):
    depth = summed.shape[-1] // 2
    half = depth // 2
    index = jnp.arange(half, dtype=jnp.int32).astype(jnp.float32)
    inverse = jnp.exp(index * (-2.0 * math.log(rope_base) / depth))
    angle = positions[..., None] * inverse
    cosine = jnp.cos(angle)[:, :, None, :]
    sine = jnp.sin(angle)[:, :, None, :]
    first = summed[..., :half]
    second = summed[..., half:depth]
    return jnp.concatenate(
        [first * cosine - second * sine, second * cosine + first * sine, summed[..., depth:]],
        axis=-1,
    )


def attend(queries, cache, fresh, lengths):
    batch, decode_steps, query_heads, depth = queries.shape
    kv_heads = cache.shape[2]
    context = cache.shape[1]
    grouped = queries.reshape(batch, decode_steps, kv_heads, query_heads // kv_heads, depth)
    scale = 1.0 / math.sqrt(depth)
    older = (
        jnp.einsum(
            "rsgqd,rpgd->rsgqp", grouped, cache[..., :depth], preferred_element_type=jnp.float32
        )
        * scale
    )
    newer = (
        jnp.einsum(
            "rsgqd,rtgd->rsgqt", grouped, fresh[..., :depth], preferred_element_type=jnp.float32
        )
        * scale
    )
    visible_old = jnp.arange(context, dtype=jnp.int32)[None, :] < lengths[:, None]
    visible_new = (
        jnp.arange(decode_steps, dtype=jnp.int32)[None, :]
        <= jnp.arange(decode_steps, dtype=jnp.int32)[:, None]
    )
    older = jnp.where(visible_old[:, None, None, None, :], older, -jnp.inf)
    newer = jnp.where(visible_new[None, :, None, None, :], newer, -jnp.inf)
    scores = jnp.concatenate([older, newer], axis=-1)
    top = jnp.max(scores, axis=-1, keepdims=True)
    weights = jnp.exp(scores - top)
    weights = (weights / jnp.sum(weights, axis=-1, keepdims=True)).astype(jnp.bfloat16)
    mixed = jnp.einsum(
        "rsgqp,rpgd->rsgqd",
        weights[..., :context],
        cache[..., depth:],
        preferred_element_type=jnp.float32,
    )
    mixed = mixed + jnp.einsum(
        "rsgqt,rtgd->rsgqd",
        weights[..., context:],
        fresh[..., depth:],
        preferred_element_type=jnp.float32,
    )
    return mixed.reshape(batch, decode_steps, query_heads, depth).astype(jnp.bfloat16)


def gather_kernel(
    n, m, tok, a, b, ids, tok_all, slices, a_all, b_all, ids_all,
    tok_v, a_v, b_v, ids_v, in_sem, own_sem, right_send, left_send, tok_recv, core_send, core_recv,
    x_send, x_recv, id_send, id_recv,
):
    f = lax.axis_index("fsdp")
    r = lax.axis_index("rows")
    t = lax.axis_index("tp")
    rows, half = tok.shape
    part = rows // CHUNKS
    width = slices.shape[2]
    per_core = half // width
    holds = t == f // per_core
    column = pl.multiple_of(lax.rem(f, per_core) * width, width)

    barrier = pltpu.get_barrier_semaphore()
    for k in range(1, n):
        pl.semaphore_signal(
            barrier, inc=1, device_id={"fsdp": lax.rem(f + k, n)}, device_id_type=MESH
        )
    for k in range(1, m):
        pl.semaphore_signal(
            barrier, inc=1, device_id={"rows": lax.rem(r + k, m)}, device_id_type=MESH
        )
    pl.semaphore_signal(barrier, inc=1, device_id={"tp": 1 - t}, device_id_type=MESH)
    pl.semaphore_wait(barrier, n + m - 1)

    def piece(c):
        return pl.ds(c * part, part)

    def along(source, src, c, to, sems):
        return pltpu.make_async_remote_copy(
            src_ref=source,
            dst_ref=tok_all.at[src, piece(c)],
            send_sem=sems.at[src, c],
            recv_sem=tok_recv.at[src, c],
            device_id={"fsdp": to},
            device_id_type=MESH,
        )

    def across(source, src, c):
        return pltpu.make_async_remote_copy(
            src_ref=source,
            dst_ref=slices.at[src, piece(c)],
            send_sem=core_send.at[src, c],
            recv_sem=core_recv.at[src, c],
            device_id={"tp": 1 - t},
            device_id_type=MESH,
        )

    def keep(source, src, c):
        return pltpu.make_async_copy(source, slices.at[src, piece(c)], core_recv.at[src, c])

    def id_copy(k):
        return pltpu.make_async_remote_copy(
            src_ref=ids,
            dst_ref=ids_all.at[f],
            send_sem=id_send.at[k],
            recv_sem=id_recv.at[k],
            device_id={"fsdp": lax.rem(f + k, n)},
            device_id_type=MESH,
        )

    def x_copy(k, which):
        source, target = ((a, a_all), (b, b_all))[which]
        return pltpu.make_async_remote_copy(
            src_ref=source,
            dst_ref=target.at[r],
            send_sem=x_send.at[which, k],
            recv_sem=x_recv.at[which, k],
            device_id={"rows": lax.rem(r + k, m)},
            device_id_type=MESH,
        )

    for c in range(CHUNKS):
        @pl.when(f < n - 1)
        def _():
            along(tok.at[piece(c)], f, c, f + 1, right_send).start()

        @pl.when(f > 0)
        def _():
            along(tok.at[piece(c)], f, c, f - 1, left_send).start()

    for k in range(1, n):
        id_copy(k).start()
    for k in range(1, m):
        for which in range(2):
            x_copy(k, which).start()
    held = ((tok, tok_v), (a, a_v), (b, b_v), (ids, ids_v))
    inward = [pltpu.make_async_copy(x, v, in_sem.at[i]) for i, (x, v) in enumerate(held)]
    for copy in inward:
        copy.start()
    locals_ = [
        pltpu.make_async_copy(tok_v, tok_all.at[f], own_sem.at[0]),
        pltpu.make_async_copy(a_v, a_all.at[r], own_sem.at[1]),
        pltpu.make_async_copy(b_v, b_all.at[r], own_sem.at[2]),
        pltpu.make_async_copy(ids_v, ids_all.at[f], own_sem.at[3]),
    ]
    for first, second in zip(inward, locals_):
        first.wait()
        second.start()
    for c in range(CHUNKS):
        @pl.when(holds)
        def _():
            across(tok.at[piece(c), pl.ds(column, width)], f, c).start()
            keep(tok_v.at[piece(c), pl.ds(column, width)], f, c).start()

    for d in range(1, n):
        for c in range(CHUNKS):
            @pl.when(f >= d)
            def _():
                src = f - d
                along(tok.at[piece(c)], src, c, f, right_send).wait_recv()

                @pl.when(f < n - 1)
                def _():
                    along(tok_all.at[src, piece(c)], src, c, f + 1, right_send).start()

                @pl.when(holds)
                def _():
                    across(tok_all.at[src, piece(c), pl.ds(column, width)], src, c).start()
                    keep(tok_all.at[src, piece(c), pl.ds(column, width)], src, c).start()

            @pl.when(f + d < n)
            def _():
                src = f + d
                along(tok.at[piece(c)], src, c, f, left_send).wait_recv()

                @pl.when(f > 0)
                def _():
                    along(tok_all.at[src, piece(c)], src, c, f - 1, left_send).start()

                @pl.when(holds)
                def _():
                    across(tok_all.at[src, piece(c), pl.ds(column, width)], src, c).start()
                    keep(tok_all.at[src, piece(c), pl.ds(column, width)], src, c).start()

    for copy in locals_:
        copy.wait()
    for k in range(1, n):
        id_copy(k).wait()
    for k in range(1, m):
        for which in range(2):
            x_copy(k, which).wait()
    for src in range(n):
        for c in range(CHUNKS):
            @pl.when(jnp.logical_and(src <= f, f < n - 1))
            def _():
                along(tok.at[piece(c)], src, c, f, right_send).wait_send()

            @pl.when(jnp.logical_and(src >= f, f > 0))
            def _():
                along(tok.at[piece(c)], src, c, f, left_send).wait_send()

            @pl.when(holds)
            def _():
                across(tok.at[piece(c), pl.ds(column, width)], src, c).wait_send()
                keep(tok.at[piece(c), pl.ds(column, width)], src, c).wait()

            @pl.when(jnp.logical_not(holds))
            def _():
                across(tok.at[piece(c), pl.ds(column, width)], src, c).wait_recv()


def gather(tok, a, b, ids, n, m, width):
    shape = jax.ShapeDtypeStruct
    anywhere = pl.BlockSpec(memory_space=pl.ANY)
    dma = pltpu.SemaphoreType.DMA
    return pl.pallas_call(
        functools.partial(gather_kernel, n, m),
        out_shape=(
            shape((n,) + tok.shape, tok.dtype),
            shape((n, tok.shape[0], width), tok.dtype),
            shape((m,) + a.shape, a.dtype),
            shape((m,) + b.shape, b.dtype),
            shape((n,) + ids.shape, ids.dtype),
        ),
        in_specs=[anywhere] * 4,
        out_specs=[anywhere] * 5,
        scratch_shapes=[pltpu.VMEM(x.shape, x.dtype) for x in (tok, a, b, ids)]
        + [
            dma((4,)),
            dma((4,)),
            dma((n, CHUNKS)),
            dma((n, CHUNKS)),
            dma((n, CHUNKS)),
            dma((n, CHUNKS)),
            dma((n, CHUNKS)),
            dma((2, m)),
            dma((2, m)),
            dma((n,)),
            dma((n,)),
        ],
        compiler_params=pltpu.CompilerParams(
            collective_id=0, has_side_effects=True, vmem_limit_bytes=32 * 2**20
        ),
    )(tok, a, b, ids)


def exchange_kernel(n, parts, out, send, recv):
    f = lax.axis_index("fsdp")
    barrier = pltpu.get_barrier_semaphore()
    for k in range(1, n):
        pl.semaphore_signal(
            barrier, inc=1, device_id={"fsdp": lax.rem(f + k, n)}, device_id_type=MESH
        )
    pl.semaphore_wait(barrier, n - 1)

    def copy(k):
        to = lax.rem(f + k, n)
        return pltpu.make_async_remote_copy(
            src_ref=parts.at[to],
            dst_ref=out.at[f],
            send_sem=send.at[k],
            recv_sem=recv.at[k],
            device_id={"fsdp": to},
            device_id_type=MESH,
        )

    for k in range(1, n):
        copy(k).start()
    for k in range(1, n):
        copy(k).wait()


def exchange(parts, n):
    anywhere = pl.BlockSpec(memory_space=pl.ANY)
    return pl.pallas_call(
        functools.partial(exchange_kernel, n),
        out_shape=jax.ShapeDtypeStruct(parts.shape, parts.dtype),
        in_specs=[anywhere],
        out_specs=anywhere,
        scratch_shapes=[pltpu.SemaphoreType.DMA((n,)), pltpu.SemaphoreType.DMA((n,))],
        compiler_params=pltpu.CompilerParams(collective_id=1, has_side_effects=True),
    )(parts)


def local(tokens, queries, kv_cache, kv_weight, adapter_a, adapter_b, adapter_id, kv_len):
    n = lax.axis_size("fsdp")
    m = lax.axis_size("rows")
    f = lax.axis_index("fsdp")
    rows_dev, decode_steps, half_width = tokens.shape
    width, heads, pair = kv_weight.shape
    rank = adapter_b.shape[2]
    count = rows_dev * decode_steps
    known = m * ADP_DEV

    flat = tokens.reshape(count, half_width)
    weight = kv_weight.reshape(width, heads * pair)
    down = adapter_a.reshape(ADP_DEV * 2 * rank, half_width)
    up = adapter_b.reshape(ADP_DEV * 2 * rank, heads * (pair // 2))
    lanes = -(-rows_dev // 128) * 128
    ids = jnp.broadcast_to(jnp.pad(adapter_id, (0, lanes - rows_dev))[None, :], (8, lanes))
    tok_all, slices, a_all, b_all, ids_all = gather(flat, down, up, ids, n, m, width)

    names = ids_all[:, 0, :rows_dev].reshape(n * rows_dev) - f * known
    chosen = names[:, None] == jnp.arange(known, dtype=jnp.int32)
    chosen = jnp.broadcast_to(chosen[:, None, :], (n * rows_dev, decode_steps, known))
    chosen = chosen.reshape(n * count, known)
    projected = lax.dot_general(
        tok_all.reshape(n * count, half_width),
        a_all.reshape(known * 2 * rank, half_width),
        (((1,), (1,)), ((), ())),
        preferred_element_type=jnp.float32,
    )
    coords = jnp.sum(
        jnp.where(chosen[:, :, None], projected.reshape(n * count, known, 2 * rank), 0.0), axis=1
    )
    coords = lax.psum(coords, "tp").astype(jnp.bfloat16)
    lane = jnp.arange(known * 2 * rank, dtype=jnp.int32)
    copies = (lane[None, :] % (2 * rank) == jnp.arange(2 * rank, dtype=jnp.int32)[:, None]).astype(
        jnp.bfloat16
    )
    token_names = jnp.broadcast_to(names[:, None], (n * rows_dev, decode_steps)).reshape(n * count)
    spread = jnp.dot(coords, copies, preferred_element_type=jnp.float32)
    spread = jnp.where(
        token_names[:, None] == lane[None, :] // (2 * rank), spread, 0.0
    ).astype(jnp.bfloat16)
    depth = pair // 2
    ups = b_all.reshape(known * 2 * rank, heads * depth)
    kind = (lane // rank % 2)[:, None]
    ups = jnp.concatenate(
        [
            jnp.where(kind == k, ups[:, h * depth : (h + 1) * depth], jnp.bfloat16(0))
            for h in range(heads)
            for k in range(2)
        ],
        axis=1,
    )
    delta = jnp.dot(spread, ups, preferred_element_type=jnp.float32)
    delta = (delta * low_rank_scale).astype(jnp.bfloat16)
    partial = jnp.dot(
        slices.reshape(n * count, width), weight, preferred_element_type=jnp.float32
    )
    parts = (partial + delta.astype(jnp.float32)).astype(jnp.bfloat16)
    parts = parts.reshape(n, count, heads * pair)
    others = exchange(parts, n)
    slot = jnp.arange(n, dtype=jnp.int32)[:, None, None]
    summed = jnp.sum(jnp.where(slot == f, parts, others).astype(jnp.float32), axis=0)
    summed = summed.reshape(rows_dev, decode_steps, heads, pair)
    positions = (kv_len[:, None] + jnp.arange(decode_steps, dtype=jnp.int32)[None, :]).astype(
        jnp.float32
    )
    new_kv = rotate_keys(summed, positions).astype(jnp.bfloat16)
    attended = attend(queries, kv_cache, new_kv, kv_len)
    return (attended, new_kv)


def solution(mesh):
    placed = (
        P(("groups", "fsdp", "rows"), None, "tp"),
        P(("groups", "fsdp", "rows"), None, "tp", None),
        P(("groups", "fsdp", "rows"), None, "tp", None),
        P("fsdp", "tp", None),
        P(("fsdp", "rows"), None, "tp"),
        P(("fsdp", "rows"), None, None, "tp", None),
        P(("groups", "fsdp", "rows")),
        P(("groups", "fsdp", "rows")),
    )
    return jax.shard_map(
        local,
        mesh=mesh,
        in_specs=placed,
        out_specs=(
            P(("groups", "fsdp", "rows"), None, "tp", None),
            P(("groups", "fsdp", "rows"), None, "tp", None),
        ),
        check_vma=False,
    )
```

```python
import functools
import math

import jax
import jax.numpy as jnp
from jax import lax
from jax.experimental import pallas as pl
from jax.experimental.pallas import tpu as pltpu
from jax.sharding import PartitionSpec as P

ADP_DEV = 16
CHUNKS = 4
MESH = pl.DeviceIdType.MESH

low_rank_scale = 0.5
rope_base = 500000.0


def rotate_keys(summed, positions):
    depth = summed.shape[-1] // 2
    half = depth // 2
    index = jnp.arange(half, dtype=jnp.int32).astype(jnp.float32)
    inverse = jnp.exp(index * (-2.0 * math.log(rope_base) / depth))
    angle = positions[..., None] * inverse
    cosine = jnp.cos(angle)[:, :, None, :]
    sine = jnp.sin(angle)[:, :, None, :]
    first = summed[..., :half]
    second = summed[..., half:depth]
    return jnp.concatenate(
        [first * cosine - second * sine, second * cosine + first * sine, summed[..., depth:]],
        axis=-1,
    )


def attend(queries, cache, fresh, lengths):
    batch, decode_steps, query_heads, depth = queries.shape
    kv_heads = cache.shape[2]
    context = cache.shape[1]
    grouped = queries.reshape(batch, decode_steps, kv_heads, query_heads // kv_heads, depth)
    scale = 1.0 / math.sqrt(depth)
    older = (
        jnp.einsum(
            "rsgqd,rpgd->rsgqp", grouped, cache[..., :depth], preferred_element_type=jnp.float32
        )
        * scale
    )
    newer = (
        jnp.einsum(
            "rsgqd,rtgd->rsgqt", grouped, fresh[..., :depth], preferred_element_type=jnp.float32
        )
        * scale
    )
    visible_old = jnp.arange(context, dtype=jnp.int32)[None, :] < lengths[:, None]
    visible_new = (
        jnp.arange(decode_steps, dtype=jnp.int32)[None, :]
        <= jnp.arange(decode_steps, dtype=jnp.int32)[:, None]
    )
    older = jnp.where(visible_old[:, None, None, None, :], older, -jnp.inf)
    newer = jnp.where(visible_new[None, :, None, None, :], newer, -jnp.inf)
    scores = jnp.concatenate([older, newer], axis=-1)
    top = jnp.max(scores, axis=-1, keepdims=True)
    weights = jnp.exp(scores - top)
    weights = (weights / jnp.sum(weights, axis=-1, keepdims=True)).astype(jnp.bfloat16)
    mixed = jnp.einsum(
        "rsgqp,rpgd->rsgqd",
        weights[..., :context],
        cache[..., depth:],
        preferred_element_type=jnp.float32,
    )
    mixed = mixed + jnp.einsum(
        "rsgqt,rtgd->rsgqd",
        weights[..., context:],
        fresh[..., depth:],
        preferred_element_type=jnp.float32,
    )
    return mixed.reshape(batch, decode_steps, query_heads, depth).astype(jnp.bfloat16)


def gather_kernel(
    n, m, tok, a, b, ids, tok_all, slices, a_all, b_all, ids_all,
    tok_v, a_v, b_v, ids_v, in_sem, own_sem, right_send, left_send, tok_recv, core_send, core_recv,
    x_send, x_recv, id_send, id_recv,
):
    f = lax.axis_index("fsdp")
    r = lax.axis_index("rows")
    t = lax.axis_index("tp")
    rows, half = tok.shape
    part = rows // CHUNKS
    width = slices.shape[2]
    per_core = half // width
    holds = t == f // per_core
    column = pl.multiple_of(lax.rem(f, per_core) * width, width)

    barrier = pltpu.get_barrier_semaphore()
    for k in range(1, n):
        pl.semaphore_signal(
            barrier, inc=1, device_id={"fsdp": lax.rem(f + k, n)}, device_id_type=MESH
        )
    for k in range(1, m):
        pl.semaphore_signal(
            barrier, inc=1, device_id={"rows": lax.rem(r + k, m)}, device_id_type=MESH
        )
    pl.semaphore_signal(barrier, inc=1, device_id={"tp": 1 - t}, device_id_type=MESH)
    pl.semaphore_wait(barrier, n + m - 1)

    def piece(c):
        return pl.ds(c * part, part)

    def along(source, src, c, to, sems):
        return pltpu.make_async_remote_copy(
            src_ref=source,
            dst_ref=tok_all.at[src, piece(c)],
            send_sem=sems.at[src, c],
            recv_sem=tok_recv.at[src, c],
            device_id={"fsdp": to},
            device_id_type=MESH,
        )

    def across(source, src, c):
        return pltpu.make_async_remote_copy(
            src_ref=source,
            dst_ref=slices.at[src, piece(c)],
            send_sem=core_send.at[src, c],
            recv_sem=core_recv.at[src, c],
            device_id={"tp": 1 - t},
            device_id_type=MESH,
        )

    def keep(source, src, c):
        return pltpu.make_async_copy(source, slices.at[src, piece(c)], core_recv.at[src, c])

    def id_copy(k):
        return pltpu.make_async_remote_copy(
            src_ref=ids,
            dst_ref=ids_all.at[f],
            send_sem=id_send.at[k],
            recv_sem=id_recv.at[k],
            device_id={"fsdp": lax.rem(f + k, n)},
            device_id_type=MESH,
        )

    def x_copy(k, which):
        source, target = ((a, a_all), (b, b_all))[which]
        return pltpu.make_async_remote_copy(
            src_ref=source,
            dst_ref=target.at[r],
            send_sem=x_send.at[which, k],
            recv_sem=x_recv.at[which, k],
            device_id={"rows": lax.rem(r + k, m)},
            device_id_type=MESH,
        )

    for c in range(CHUNKS):
        @pl.when(f < n - 1)
        def _():
            along(tok.at[piece(c)], f, c, f + 1, right_send).start()

        @pl.when(f > 0)
        def _():
            along(tok.at[piece(c)], f, c, f - 1, left_send).start()

    for k in range(1, n):
        id_copy(k).start()
    for k in range(1, m):
        for which in range(2):
            x_copy(k, which).start()
    held = ((tok, tok_v), (a, a_v), (b, b_v), (ids, ids_v))
    inward = [pltpu.make_async_copy(x, v, in_sem.at[i]) for i, (x, v) in enumerate(held)]
    for copy in inward:
        copy.start()
    locals_ = [
        pltpu.make_async_copy(tok_v, tok_all.at[f], own_sem.at[0]),
        pltpu.make_async_copy(a_v, a_all.at[r], own_sem.at[1]),
        pltpu.make_async_copy(b_v, b_all.at[r], own_sem.at[2]),
        pltpu.make_async_copy(ids_v, ids_all.at[f], own_sem.at[3]),
    ]
    for first, second in zip(inward, locals_):
        first.wait()
        second.start()
    for c in range(CHUNKS):
        @pl.when(holds)
        def _():
            across(tok.at[piece(c), pl.ds(column, width)], f, c).start()
            keep(tok_v.at[piece(c), pl.ds(column, width)], f, c).start()

    for d in range(1, n):
        for c in range(CHUNKS):
            @pl.when(f >= d)
            def _():
                src = f - d
                along(tok.at[piece(c)], src, c, f, right_send).wait_recv()

                @pl.when(f < n - 1)
                def _():
                    along(tok_all.at[src, piece(c)], src, c, f + 1, right_send).start()

                @pl.when(holds)
                def _():
                    across(tok_all.at[src, piece(c), pl.ds(column, width)], src, c).start()
                    keep(tok_all.at[src, piece(c), pl.ds(column, width)], src, c).start()

            @pl.when(f + d < n)
            def _():
                src = f + d
                along(tok.at[piece(c)], src, c, f, left_send).wait_recv()

                @pl.when(f > 0)
                def _():
                    along(tok_all.at[src, piece(c)], src, c, f - 1, left_send).start()

                @pl.when(holds)
                def _():
                    across(tok_all.at[src, piece(c), pl.ds(column, width)], src, c).start()
                    keep(tok_all.at[src, piece(c), pl.ds(column, width)], src, c).start()

    for copy in locals_:
        copy.wait()
    for k in range(1, n):
        id_copy(k).wait()
    for k in range(1, m):
        for which in range(2):
            x_copy(k, which).wait()
    for src in range(n):
        for c in range(CHUNKS):
            @pl.when(jnp.logical_and(src <= f, f < n - 1))
            def _():
                along(tok.at[piece(c)], src, c, f, right_send).wait_send()

            @pl.when(jnp.logical_and(src >= f, f > 0))
            def _():
                along(tok.at[piece(c)], src, c, f, left_send).wait_send()

            @pl.when(holds)
            def _():
                across(tok.at[piece(c), pl.ds(column, width)], src, c).wait_send()
                keep(tok.at[piece(c), pl.ds(column, width)], src, c).wait()

            @pl.when(jnp.logical_not(holds))
            def _():
                across(tok.at[piece(c), pl.ds(column, width)], src, c).wait_recv()


def gather(tok, a, b, ids, n, m, width):
    shape = jax.ShapeDtypeStruct
    anywhere = pl.BlockSpec(memory_space=pl.ANY)
    dma = pltpu.SemaphoreType.DMA
    return pl.pallas_call(
        functools.partial(gather_kernel, n, m),
        out_shape=(
            shape((n,) + tok.shape, tok.dtype),
            shape((n, tok.shape[0], width), tok.dtype),
            shape((m,) + a.shape, a.dtype),
            shape((m,) + b.shape, b.dtype),
            shape((n,) + ids.shape, ids.dtype),
        ),
        in_specs=[anywhere] * 4,
        out_specs=[anywhere] * 5,
        scratch_shapes=[pltpu.VMEM(x.shape, x.dtype) for x in (tok, a, b, ids)]
        + [
            dma((4,)),
            dma((4,)),
            dma((n, CHUNKS)),
            dma((n, CHUNKS)),
            dma((n, CHUNKS)),
            dma((n, CHUNKS)),
            dma((n, CHUNKS)),
            dma((2, m)),
            dma((2, m)),
            dma((n,)),
            dma((n,)),
        ],
        compiler_params=pltpu.CompilerParams(
            collective_id=0, has_side_effects=True, vmem_limit_bytes=32 * 2**20
        ),
    )(tok, a, b, ids)


def exchange(parts, f, n):
    total = lax.dynamic_index_in_dim(parts, f, 0, keepdims=False).astype(jnp.float32)
    for k in range(1, n):
        leaving = lax.dynamic_index_in_dim(parts, lax.rem(f + k, n), 0, keepdims=False)
        arrived = lax.ppermute(leaving, "fsdp", [(i, (i + k) % n) for i in range(n)])
        total = total + arrived.astype(jnp.float32)
    return total


def local(tokens, queries, kv_cache, kv_weight, adapter_a, adapter_b, adapter_id, kv_len):
    n = lax.axis_size("fsdp")
    m = lax.axis_size("rows")
    f = lax.axis_index("fsdp")
    rows_dev, decode_steps, half_width = tokens.shape
    width, heads, pair = kv_weight.shape
    rank = adapter_b.shape[2]
    count = rows_dev * decode_steps
    known = m * ADP_DEV

    flat = tokens.reshape(count, half_width)
    weight = kv_weight.reshape(width, heads * pair)
    down = adapter_a.reshape(ADP_DEV * 2 * rank, half_width)
    up = adapter_b.reshape(ADP_DEV * 2 * rank, heads * (pair // 2))
    lanes = -(-rows_dev // 128) * 128
    ids = jnp.broadcast_to(jnp.pad(adapter_id, (0, lanes - rows_dev))[None, :], (8, lanes))
    tok_all, slices, a_all, b_all, ids_all = gather(flat, down, up, ids, n, m, width)

    names = ids_all[:, 0, :rows_dev].reshape(n * rows_dev) - f * known
    chosen = names[:, None] == jnp.arange(known, dtype=jnp.int32)
    chosen = jnp.broadcast_to(chosen[:, None, :], (n * rows_dev, decode_steps, known))
    chosen = chosen.reshape(n * count, known)
    projected = lax.dot_general(
        tok_all.reshape(n * count, half_width),
        a_all.reshape(known * 2 * rank, half_width),
        (((1,), (1,)), ((), ())),
        preferred_element_type=jnp.float32,
    )
    coords = jnp.sum(
        jnp.where(chosen[:, :, None], projected.reshape(n * count, known, 2 * rank), 0.0), axis=1
    )
    coords = lax.psum(coords, "tp").astype(jnp.bfloat16)
    lane = jnp.arange(known * 2 * rank, dtype=jnp.int32)
    copies = (lane[None, :] % (2 * rank) == jnp.arange(2 * rank, dtype=jnp.int32)[:, None]).astype(
        jnp.bfloat16
    )
    token_names = jnp.broadcast_to(names[:, None], (n * rows_dev, decode_steps)).reshape(n * count)
    spread = jnp.dot(coords, copies, preferred_element_type=jnp.float32)
    spread = jnp.where(
        token_names[:, None] == lane[None, :] // (2 * rank), spread, 0.0
    ).astype(jnp.bfloat16)
    depth = pair // 2
    ups = b_all.reshape(known * 2 * rank, heads * depth)
    kind = (lane // rank % 2)[:, None]
    ups = jnp.concatenate(
        [
            jnp.where(kind == k, ups[:, h * depth : (h + 1) * depth], jnp.bfloat16(0))
            for h in range(heads)
            for k in range(2)
        ],
        axis=1,
    )
    delta = jnp.dot(spread, ups, preferred_element_type=jnp.float32)
    delta = (delta * low_rank_scale).astype(jnp.bfloat16)
    partial = jnp.dot(
        slices.reshape(n * count, width), weight, preferred_element_type=jnp.float32
    )
    parts = (partial + delta.astype(jnp.float32)).astype(jnp.bfloat16)
    parts = parts.reshape(n, count, heads * pair)
    summed = exchange(parts, f, n)
    summed = summed.reshape(rows_dev, decode_steps, heads, pair)
    positions = (kv_len[:, None] + jnp.arange(decode_steps, dtype=jnp.int32)[None, :]).astype(
        jnp.float32
    )
    new_kv = rotate_keys(summed, positions).astype(jnp.bfloat16)
    attended = attend(queries, kv_cache, new_kv, kv_len)
    return (attended, new_kv)


def solution(mesh):
    placed = (
        P(("groups", "fsdp", "rows"), None, "tp"),
        P(("groups", "fsdp", "rows"), None, "tp", None),
        P(("groups", "fsdp", "rows"), None, "tp", None),
        P("fsdp", "tp", None),
        P(("fsdp", "rows"), None, "tp"),
        P(("fsdp", "rows"), None, None, "tp", None),
        P(("groups", "fsdp", "rows")),
        P(("groups", "fsdp", "rows")),
    )
    return jax.shard_map(
        local,
        mesh=mesh,
        in_specs=placed,
        out_specs=(
            P(("groups", "fsdp", "rows"), None, "tp", None),
            P(("groups", "fsdp", "rows"), None, "tp", None),
        ),
        check_vma=False,
    )
```

```python
import functools
import math

import jax
import jax.numpy as jnp
from jax import lax
from jax.experimental import pallas as pl
from jax.experimental.pallas import tpu as pltpu
from jax.sharding import PartitionSpec as P

ADP_DEV = 16
CHUNKS = 6
MESH = pl.DeviceIdType.MESH

low_rank_scale = 0.5
rope_base = 500000.0


def rotate_keys(summed, positions):
    depth = summed.shape[-1] // 2
    half = depth // 2
    index = jnp.arange(half, dtype=jnp.int32).astype(jnp.float32)
    inverse = jnp.exp(index * (-2.0 * math.log(rope_base) / depth))
    angle = positions[..., None] * inverse
    cosine = jnp.cos(angle)[:, :, None, :]
    sine = jnp.sin(angle)[:, :, None, :]
    first = summed[..., :half]
    second = summed[..., half:depth]
    return jnp.concatenate(
        [first * cosine - second * sine, second * cosine + first * sine, summed[..., depth:]],
        axis=-1,
    )


def attend(queries, cache, fresh, lengths):
    batch, decode_steps, query_heads, depth = queries.shape
    kv_heads = cache.shape[2]
    context = cache.shape[1]
    grouped = queries.reshape(batch, decode_steps, kv_heads, query_heads // kv_heads, depth)
    scale = 1.0 / math.sqrt(depth)
    older = (
        jnp.einsum(
            "rsgqd,rpgd->rsgqp", grouped, cache[..., :depth], preferred_element_type=jnp.float32
        )
        * scale
    )
    newer = (
        jnp.einsum(
            "rsgqd,rtgd->rsgqt", grouped, fresh[..., :depth], preferred_element_type=jnp.float32
        )
        * scale
    )
    visible_old = jnp.arange(context, dtype=jnp.int32)[None, :] < lengths[:, None]
    visible_new = (
        jnp.arange(decode_steps, dtype=jnp.int32)[None, :]
        <= jnp.arange(decode_steps, dtype=jnp.int32)[:, None]
    )
    older = jnp.where(visible_old[:, None, None, None, :], older, -jnp.inf)
    newer = jnp.where(visible_new[None, :, None, None, :], newer, -jnp.inf)
    scores = jnp.concatenate([older, newer], axis=-1)
    top = jnp.max(scores, axis=-1, keepdims=True)
    weights = jnp.exp(scores - top)
    weights = (weights / jnp.sum(weights, axis=-1, keepdims=True)).astype(jnp.bfloat16)
    mixed = jnp.einsum(
        "rsgqp,rpgd->rsgqd",
        weights[..., :context],
        cache[..., depth:],
        preferred_element_type=jnp.float32,
    )
    mixed = mixed + jnp.einsum(
        "rsgqt,rtgd->rsgqd",
        weights[..., context:],
        fresh[..., depth:],
        preferred_element_type=jnp.float32,
    )
    return mixed.reshape(batch, decode_steps, query_heads, depth).astype(jnp.bfloat16)


def gather_kernel(
    n, m, tok, a, b, ids, tok_all, slices, a_all, b_all, ids_all,
    tok_v, a_v, b_v, ids_v, in_sem, own_sem, right_send, left_send, tok_recv, core_send, core_recv,
    x_send, x_recv, id_send, id_recv,
):
    f = lax.axis_index("fsdp")
    r = lax.axis_index("rows")
    t = lax.axis_index("tp")
    rows, half = tok.shape
    part = rows // CHUNKS
    width = slices.shape[2]
    per_core = half // width
    holds = t == f // per_core
    column = pl.multiple_of(lax.rem(f, per_core) * width, width)

    barrier = pltpu.get_barrier_semaphore()
    for k in range(1, n):
        pl.semaphore_signal(
            barrier, inc=1, device_id={"fsdp": lax.rem(f + k, n)}, device_id_type=MESH
        )
    for k in range(1, m):
        pl.semaphore_signal(
            barrier, inc=1, device_id={"rows": lax.rem(r + k, m)}, device_id_type=MESH
        )
    pl.semaphore_signal(barrier, inc=1, device_id={"tp": 1 - t}, device_id_type=MESH)
    pl.semaphore_wait(barrier, n + m - 1)

    def piece(c):
        return pl.ds(c * part, part)

    def along(source, src, c, to, sems):
        return pltpu.make_async_remote_copy(
            src_ref=source,
            dst_ref=tok_all.at[src, piece(c)],
            send_sem=sems.at[src, c],
            recv_sem=tok_recv.at[src, c],
            device_id={"fsdp": to},
            device_id_type=MESH,
        )

    def across(source, src, c):
        return pltpu.make_async_remote_copy(
            src_ref=source,
            dst_ref=slices.at[src, piece(c)],
            send_sem=core_send.at[src, c],
            recv_sem=core_recv.at[src, c],
            device_id={"tp": 1 - t},
            device_id_type=MESH,
        )

    def keep(source, src, c):
        return pltpu.make_async_copy(source, slices.at[src, piece(c)], core_recv.at[src, c])

    def id_copy(k):
        return pltpu.make_async_remote_copy(
            src_ref=ids,
            dst_ref=ids_all.at[f],
            send_sem=id_send.at[k],
            recv_sem=id_recv.at[k],
            device_id={"fsdp": lax.rem(f + k, n)},
            device_id_type=MESH,
        )

    def x_copy(k, which):
        source, target = ((a, a_all), (b, b_all))[which]
        return pltpu.make_async_remote_copy(
            src_ref=source,
            dst_ref=target.at[r],
            send_sem=x_send.at[which, k],
            recv_sem=x_recv.at[which, k],
            device_id={"rows": lax.rem(r + k, m)},
            device_id_type=MESH,
        )

    for c in range(CHUNKS):
        @pl.when(f < n - 1)
        def _():
            along(tok.at[piece(c)], f, c, f + 1, right_send).start()

        @pl.when(f > 0)
        def _():
            along(tok.at[piece(c)], f, c, f - 1, left_send).start()

    for k in range(1, n):
        id_copy(k).start()
    for k in range(1, m):
        for which in range(2):
            x_copy(k, which).start()
    held = ((tok, tok_v), (a, a_v), (b, b_v), (ids, ids_v))
    inward = [pltpu.make_async_copy(x, v, in_sem.at[i]) for i, (x, v) in enumerate(held)]
    for copy in inward:
        copy.start()
    locals_ = [
        pltpu.make_async_copy(tok_v, tok_all.at[f], own_sem.at[0]),
        pltpu.make_async_copy(a_v, a_all.at[r], own_sem.at[1]),
        pltpu.make_async_copy(b_v, b_all.at[r], own_sem.at[2]),
        pltpu.make_async_copy(ids_v, ids_all.at[f], own_sem.at[3]),
    ]
    for first, second in zip(inward, locals_):
        first.wait()
        second.start()
    for c in range(CHUNKS):
        @pl.when(holds)
        def _():
            across(tok.at[piece(c), pl.ds(column, width)], f, c).start()
            keep(tok_v.at[piece(c), pl.ds(column, width)], f, c).start()

    for d in range(1, n):
        for c in range(CHUNKS):
            @pl.when(f >= d)
            def _():
                src = f - d
                along(tok.at[piece(c)], src, c, f, right_send).wait_recv()

                @pl.when(f < n - 1)
                def _():
                    along(tok_all.at[src, piece(c)], src, c, f + 1, right_send).start()

                @pl.when(holds)
                def _():
                    across(tok_all.at[src, piece(c), pl.ds(column, width)], src, c).start()
                    keep(tok_all.at[src, piece(c), pl.ds(column, width)], src, c).start()

            @pl.when(f + d < n)
            def _():
                src = f + d
                along(tok.at[piece(c)], src, c, f, left_send).wait_recv()

                @pl.when(f > 0)
                def _():
                    along(tok_all.at[src, piece(c)], src, c, f - 1, left_send).start()

                @pl.when(holds)
                def _():
                    across(tok_all.at[src, piece(c), pl.ds(column, width)], src, c).start()
                    keep(tok_all.at[src, piece(c), pl.ds(column, width)], src, c).start()

    for copy in locals_:
        copy.wait()
    for k in range(1, n):
        id_copy(k).wait()
    for k in range(1, m):
        for which in range(2):
            x_copy(k, which).wait()
    for src in range(n):
        for c in range(CHUNKS):
            @pl.when(jnp.logical_and(src <= f, f < n - 1))
            def _():
                along(tok.at[piece(c)], src, c, f, right_send).wait_send()

            @pl.when(jnp.logical_and(src >= f, f > 0))
            def _():
                along(tok.at[piece(c)], src, c, f, left_send).wait_send()

            @pl.when(holds)
            def _():
                across(tok.at[piece(c), pl.ds(column, width)], src, c).wait_send()
                keep(tok.at[piece(c), pl.ds(column, width)], src, c).wait()

            @pl.when(jnp.logical_not(holds))
            def _():
                across(tok.at[piece(c), pl.ds(column, width)], src, c).wait_recv()


def gather(tok, a, b, ids, n, m, width):
    shape = jax.ShapeDtypeStruct
    anywhere = pl.BlockSpec(memory_space=pl.ANY)
    dma = pltpu.SemaphoreType.DMA
    return pl.pallas_call(
        functools.partial(gather_kernel, n, m),
        out_shape=(
            shape((n,) + tok.shape, tok.dtype),
            shape((n, tok.shape[0], width), tok.dtype),
            shape((m,) + a.shape, a.dtype),
            shape((m,) + b.shape, b.dtype),
            shape((n,) + ids.shape, ids.dtype),
        ),
        in_specs=[anywhere] * 4,
        out_specs=[anywhere] * 5,
        scratch_shapes=[pltpu.VMEM(x.shape, x.dtype) for x in (tok, a, b, ids)]
        + [
            dma((4,)),
            dma((4,)),
            dma((n, CHUNKS)),
            dma((n, CHUNKS)),
            dma((n, CHUNKS)),
            dma((n, CHUNKS)),
            dma((n, CHUNKS)),
            dma((2, m)),
            dma((2, m)),
            dma((n,)),
            dma((n,)),
        ],
        compiler_params=pltpu.CompilerParams(
            collective_id=0, has_side_effects=True, vmem_limit_bytes=32 * 2**20
        ),
    )(tok, a, b, ids)


def exchange_kernel(n, parts, out, send, recv):
    f = lax.axis_index("fsdp")
    barrier = pltpu.get_barrier_semaphore()
    for k in range(1, n):
        pl.semaphore_signal(
            barrier, inc=1, device_id={"fsdp": lax.rem(f + k, n)}, device_id_type=MESH
        )
    pl.semaphore_wait(barrier, n - 1)

    def copy(k):
        to = lax.rem(f + k, n)
        return pltpu.make_async_remote_copy(
            src_ref=parts.at[to],
            dst_ref=out.at[f],
            send_sem=send.at[k],
            recv_sem=recv.at[k],
            device_id={"fsdp": to},
            device_id_type=MESH,
        )

    for k in range(1, n):
        copy(k).start()
    for k in range(1, n):
        copy(k).wait()


def exchange(parts, n):
    anywhere = pl.BlockSpec(memory_space=pl.ANY)
    return pl.pallas_call(
        functools.partial(exchange_kernel, n),
        out_shape=jax.ShapeDtypeStruct(parts.shape, parts.dtype),
        in_specs=[anywhere],
        out_specs=anywhere,
        scratch_shapes=[pltpu.SemaphoreType.DMA((n,)), pltpu.SemaphoreType.DMA((n,))],
        compiler_params=pltpu.CompilerParams(collective_id=1, has_side_effects=True),
    )(parts)


def local(tokens, queries, kv_cache, kv_weight, adapter_a, adapter_b, adapter_id, kv_len):
    n = lax.axis_size("fsdp")
    m = lax.axis_size("rows")
    f = lax.axis_index("fsdp")
    rows_dev, decode_steps, half_width = tokens.shape
    width, heads, pair = kv_weight.shape
    rank = adapter_b.shape[2]
    count = rows_dev * decode_steps
    known = m * ADP_DEV

    flat = tokens.reshape(count, half_width)
    weight = kv_weight.reshape(width, heads * pair)
    down = adapter_a.reshape(ADP_DEV * 2 * rank, half_width)
    up = adapter_b.reshape(ADP_DEV * 2 * rank, heads * (pair // 2))
    lanes = -(-rows_dev // 128) * 128
    ids = jnp.broadcast_to(jnp.pad(adapter_id, (0, lanes - rows_dev))[None, :], (8, lanes))
    tok_all, slices, a_all, b_all, ids_all = gather(flat, down, up, ids, n, m, width)

    names = ids_all[:, 0, :rows_dev].reshape(n * rows_dev) - f * known
    chosen = names[:, None] == jnp.arange(known, dtype=jnp.int32)
    chosen = jnp.broadcast_to(chosen[:, None, :], (n * rows_dev, decode_steps, known))
    chosen = chosen.reshape(n * count, known)
    projected = lax.dot_general(
        tok_all.reshape(n * count, half_width),
        a_all.reshape(known * 2 * rank, half_width),
        (((1,), (1,)), ((), ())),
        preferred_element_type=jnp.float32,
    )
    coords = jnp.sum(
        jnp.where(chosen[:, :, None], projected.reshape(n * count, known, 2 * rank), 0.0), axis=1
    )
    coords = lax.psum(coords, "tp").astype(jnp.bfloat16)
    lane = jnp.arange(known * 2 * rank, dtype=jnp.int32)
    copies = (lane[None, :] % (2 * rank) == jnp.arange(2 * rank, dtype=jnp.int32)[:, None]).astype(
        jnp.bfloat16
    )
    token_names = jnp.broadcast_to(names[:, None], (n * rows_dev, decode_steps)).reshape(n * count)
    spread = jnp.dot(coords, copies, preferred_element_type=jnp.float32)
    spread = jnp.where(
        token_names[:, None] == lane[None, :] // (2 * rank), spread, 0.0
    ).astype(jnp.bfloat16)
    depth = pair // 2
    ups = b_all.reshape(known * 2 * rank, heads * depth)
    kind = (lane // rank % 2)[:, None]
    ups = jnp.concatenate(
        [
            jnp.where(kind == k, ups[:, h * depth : (h + 1) * depth], jnp.bfloat16(0))
            for h in range(heads)
            for k in range(2)
        ],
        axis=1,
    )
    delta = jnp.dot(spread, ups, preferred_element_type=jnp.float32)
    delta = (delta * low_rank_scale).astype(jnp.bfloat16)
    partial = jnp.dot(
        slices.reshape(n * count, width), weight, preferred_element_type=jnp.float32
    )
    parts = (partial + delta.astype(jnp.float32)).astype(jnp.bfloat16)
    parts = parts.reshape(n, count, heads * pair)
    others = exchange(parts, n)
    slot = jnp.arange(n, dtype=jnp.int32)[:, None, None]
    summed = jnp.sum(jnp.where(slot == f, parts, others).astype(jnp.float32), axis=0)
    summed = summed.reshape(rows_dev, decode_steps, heads, pair)
    positions = (kv_len[:, None] + jnp.arange(decode_steps, dtype=jnp.int32)[None, :]).astype(
        jnp.float32
    )
    new_kv = rotate_keys(summed, positions).astype(jnp.bfloat16)
    attended = attend(queries, kv_cache, new_kv, kv_len)
    return (attended, new_kv)


def solution(mesh):
    placed = (
        P(("groups", "fsdp", "rows"), None, "tp"),
        P(("groups", "fsdp", "rows"), None, "tp", None),
        P(("groups", "fsdp", "rows"), None, "tp", None),
        P("fsdp", "tp", None),
        P(("fsdp", "rows"), None, "tp"),
        P(("fsdp", "rows"), None, None, "tp", None),
        P(("groups", "fsdp", "rows")),
        P(("groups", "fsdp", "rows")),
    )
    return jax.shard_map(
        local,
        mesh=mesh,
        in_specs=placed,
        out_specs=(
            P(("groups", "fsdp", "rows"), None, "tp", None),
            P(("groups", "fsdp", "rows"), None, "tp", None),
        ),
        check_vma=False,
    )
```
